32 devices in a mesh: rep: 2 (over x), grp: 8 (over z, y), head: 2 (over core).
Axes of the slice: x: 2, y: 2, z: 4, core: 2. Of those that a mesh axis runs over, the one named last changes fastest.
Arguments:
- queries: bfloat16 [2048, 2560], P(('rep', 'grp'), 'head'), parts along dimension 0, may hold values from -180 to 180
- key_matrix: bfloat16 [2048, 512], P(('rep', 'grp'), 'head'), parts along dimension 0, may hold values from -5 to 5
- value_matrix: bfloat16 [2048, 512], P(('rep', 'grp'), 'head'), parts along dimension 0, may hold values from -5 to 5
- residual: bfloat16 [2048, 2560], P(('rep', 'grp', 'head')), parts along dimension 0, may hold values from -10 to 10
- norm_gain: bfloat16 [2560], replicated, may hold values from 0.099609375 to 1.8984375
- w_gate: bfloat16 [8, 2560, 4096], P('grp', None, 'head'), may hold values from -0.125 to 0.125
- w_up: bfloat16 [8, 2560, 4096], P('grp', None, 'head'), may hold values from -0.125 to 0.125
- w_down: bfloat16 [8, 4096, 2560], P('grp', 'head'), may hold values from -0.0625 to 0.0625
- owner_class: int32 [8], replicated, may hold values from 0 to 3, as said below
- class_counts: int32 [32, 4], P(('rep', 'grp', 'head')), parts along dimension 0, may hold values from 0 to 24, as said below
- episode_index: int32 [2048], P(('rep', 'grp')), parts along dimension 0, may hold values from 0 to 1022, as said below
Outputs:
- layer_out: bfloat16 [2048, 2560], P(('rep', 'grp', 'head')), parts along dimension 0
The draws below stay inside these ranges and needn't reach their ends.
There are 2 independent parts, one for each index of `rep`. The reference program is written for one: setup_inputs(seed, part) draws one part's arguments, and reference() takes and returns one part's arrays. A program takes and returns all parts, laid end to end along the dimension named above; an argument that names none is the same for every part. Nothing has to cross between parts.
Inputs may be any that keep to these rules, and one draw needn't show every extreme that they name: `owner_class`: each class is owned by exactly 2 groups. `class_counts`: each row sums to 64; every count is even; in each draw one class has exactly 24 tokens on every device. `episode_index`: an episode's id is the index of its first token; ids never fall along the tokens; an episode begins at an even row and never spans two class runs or two shards of 64 rows.
All inputs are finite; a program needn't handle non-finite values.
Results may differ from the reference program's by a relative error of at most 0.0067.
Values may be sent and summed in bfloat16 or wider, within the bound.
A program may use at most 128 MiB of HBM per device.

```python
import math
import jax
import jax.numpy as jnp
from jax import lax

QUERY_HEADS = 20
KEY_VALUE_HEADS = 4
HEAD_SIZE = 128
D = 2560
FF = 8192
CLASSES = 4
GROUP_TOKENS = 128
TOK_H = 64
CAP = 24
TOKEN_TOTAL = 1024
N_GRP = 8
N_HEAD = 2


def layout_tables(key):
    base = jax.random.fold_in(key, 11)
    key_hot, key_fill, key_cut = jax.random.split(base, 3)
    halves = TOKEN_TOTAL // TOK_H
    hottest = jax.random.randint(key_hot, (), 0, CLASSES)
    limit = CAP // 2
    remain = jnp.full((halves,), (TOK_H - CAP) // 2, jnp.int32)
    fill_keys = jax.random.split(key_fill, CLASSES - 1)
    picked = []
    for number in range(CLASSES - 1):
        later = CLASSES - 2 - number
        lowest = jnp.maximum(remain - later * limit, 0)
        highest = jnp.minimum(remain, limit)
        chosen = jax.random.randint(fill_keys[number], (halves,), lowest, highest + 1)
        picked.append(chosen)
        remain = remain - chosen
    others = 2 * jnp.stack(picked, axis=1)
    class_range = jnp.arange(CLASSES)
    position = jnp.clip(class_range - (class_range > hottest).astype(jnp.int32), 0, CLASSES - 2)
    counts = jnp.where(class_range[None, :] == hottest, CAP, jnp.take(others, position, axis=1)).astype(jnp.int32)
    run_ends = jnp.cumsum(counts, axis=1)
    starts = run_ends - counts
    offsets = jnp.arange(TOK_H)
    begins = jnp.any((starts[:, None, :] == offsets[None, :, None]) & (counts[:, None, :] > 0), axis=2)
    extra = jax.random.randint(key_cut, (halves, TOK_H), 0, 8) == 0
    extra = extra & (offsets[None, :] % 2 == 0)
    flags = (begins | extra).reshape(-1)
    rows_all = jnp.arange(TOKEN_TOTAL).astype(jnp.int32)
    flags = flags | (rows_all == TOKEN_TOTAL - 2)
    segments = lax.cummax(jnp.where(flags, rows_all, 0).astype(jnp.int32), axis=0)
    return (counts, segments.astype(jnp.int32))


def draw_class_counts(key, part):
    return layout_tables(key)[0]


def draw_episode_index(key, part):
    return layout_tables(key)[1]


def draw_owner_class(key, part):
    return (jax.random.permutation(jax.random.fold_in(key, 5), N_GRP) % CLASSES).astype(jnp.int32)


def attention_tables(key):
    base = jax.random.fold_in(key, 23)
    key_initial, key_second = jax.random.split(base, 2)
    key_array = jnp.clip(jax.random.normal(key_initial, (TOKEN_TOTAL, KEY_VALUE_HEADS * HEAD_SIZE), jnp.float32), -5.0, 5.0)
    query_field = jnp.clip(jax.random.normal(key_second, (TOKEN_TOTAL, QUERY_HEADS * HEAD_SIZE), jnp.float32), -5.0, 5.0)
    return (query_field, key_array)


def draw_queries(key, part):
    return attention_tables(key)[0].astype(jnp.bfloat16)


def draw_key_matrix(key, part):
    return attention_tables(key)[1].astype(jnp.bfloat16)


def draw_residual(key, part):
    key_base, key_column = jax.random.split(jax.random.fold_in(key, 31), 2)
    normal_field = jnp.clip(jax.random.normal(key_base, (TOKEN_TOTAL, D), jnp.float32), -5.0, 5.0)
    column = jnp.exp(jax.random.uniform(key_column, (1, D), jnp.float32, math.log(0.1), 0.0))
    return (normal_field * column).astype(jnp.bfloat16)


def shard_levels(key, shape, pieces, least, top_value):
    level, own = 1.0, jax.random.fold_in(key, 6)
    for dim, shards_of in pieces:
        draws = jnp.exp(jax.random.uniform(jax.random.fold_in(own, dim), (shards_of,), jnp.float32, least / len(pieces), top_value / len(pieces)))
        level = level * jnp.repeat(draws, shape[dim] // shards_of).reshape([-1 if axis == dim else 1 for axis in range(len(shape))])
    return level


def gaussian(own_key, shape, width, reach, pieces=(), dtype=jnp.bfloat16):
    result = jax.random.normal(own_key, shape, jnp.float32) * width
    if len(pieces) > 0:
        result = shard_levels(own_key, shape, pieces, -0.22, 0.18) * result
    return jnp.clip(result, min=-reach, max=reach).astype(dtype)


def setup_inputs(seed: int = 0, part: int = 0) -> dict:
    arg_keys = jax.random.split(jax.random.key(seed), 12)
    own_keys = jax.random.split(jax.random.fold_in(arg_keys[11], part), 12)
    queries = draw_queries(jax.random.fold_in(jax.random.fold_in(arg_keys[11], part), 71), part)
    key_matrix = draw_key_matrix(jax.random.fold_in(jax.random.fold_in(arg_keys[11], part), 71), part)
    value_matrix = gaussian(own_keys[2], (TOKEN_TOTAL, KEY_VALUE_HEADS * HEAD_SIZE), 1.0, 5.0, ((0, 8), (1, 2)))
    residual = draw_residual(jax.random.fold_in(jax.random.fold_in(arg_keys[11], part), 71), part)
    norm_gain = jnp.clip(1.0 + 0.18 * jax.random.normal(arg_keys[4], (D,), jnp.float32), 0.099609375, 1.8984375).astype(jnp.bfloat16)
    w_gate = gaussian(arg_keys[5], (N_GRP, D, FF * CLASSES // N_GRP), D ** -0.5, 0.125, ((0, 8), (2, 2)))
    w_up = gaussian(arg_keys[6], (N_GRP, D, FF * CLASSES // N_GRP), D ** -0.5, 0.125, ((0, 8), (2, 2)))
    w_down = gaussian(arg_keys[7], (N_GRP, FF * CLASSES // N_GRP, D), FF ** -0.5, 0.0625, ((0, 8), (1, 2)))
    owner_class = draw_owner_class(jax.random.fold_in(arg_keys[11], 71), part)
    class_counts = draw_class_counts(jax.random.fold_in(jax.random.fold_in(arg_keys[11], part), 71), part)
    episode_index = draw_episode_index(jax.random.fold_in(jax.random.fold_in(arg_keys[11], part), 71), part)
    return dict(queries=queries, key_matrix=key_matrix, value_matrix=value_matrix, residual=residual, norm_gain=norm_gain, w_gate=w_gate, w_up=w_up, w_down=w_down, owner_class=owner_class, class_counts=class_counts, episode_index=episode_index)


def precise_attention(queries, key_matrix, value_matrix, episode_index):
    length = queries.shape[0]
    kv_count = key_matrix.shape[1] // HEAD_SIZE
    head_repeats = queries.shape[1] // key_matrix.shape[1]
    query_tiles = queries.reshape(length, kv_count, head_repeats, HEAD_SIZE).astype(jnp.float32)
    key_tiles = key_matrix.reshape(length, kv_count, HEAD_SIZE).astype(jnp.float32)
    value_tiles = value_matrix.reshape(length, kv_count, HEAD_SIZE).astype(jnp.float32)
    logit_table = jnp.einsum('envh,ynh->nvey', query_tiles, key_tiles) * (1.0 / math.sqrt(HEAD_SIZE))
    places = jnp.arange(length)
    allowed = (episode_index[:, None] == episode_index[None, :]) & (places[None, :] <= places[:, None])
    logit_table = jnp.where(allowed, logit_table, -jnp.inf)
    softmax_probs = jax.nn.softmax(logit_table, axis=-1).astype(jnp.bfloat16)
    mixed_values = jnp.einsum('alwn,nam->walm', softmax_probs.astype(jnp.float32), value_tiles)
    return mixed_values.reshape(length, kv_count * head_repeats * HEAD_SIZE).astype(jnp.bfloat16)

def normalize(mixed_values, norm_gain):
    square = lax.optimization_barrier(jnp.mean(mixed_values * mixed_values, axis=-1, keepdims=True))
    return (mixed_values * lax.rsqrt(square + 1e-06) * norm_gain.astype(jnp.float32)).astype(jnp.bfloat16)

def reference(queries, key_matrix, value_matrix, residual, norm_gain, w_gate, w_up, w_down, owner_class, class_counts, episode_index):
    group_count = TOKEN_TOTAL // GROUP_TOKENS
    attention_output = lax.map(lambda compact_rows: precise_attention(compact_rows[0], compact_rows[1], compact_rows[2], compact_rows[3]), (queries.reshape(group_count, GROUP_TOKENS, QUERY_HEADS * HEAD_SIZE), key_matrix.reshape(group_count, GROUP_TOKENS, KEY_VALUE_HEADS * HEAD_SIZE), value_matrix.reshape(group_count, GROUP_TOKENS, KEY_VALUE_HEADS * HEAD_SIZE), episode_index.reshape(group_count, GROUP_TOKENS)))
    attention_output = attention_output.reshape(TOKEN_TOTAL, D)
    mixed_values = residual.astype(jnp.float32) + attention_output.astype(jnp.float32)
    normed = normalize(mixed_values, norm_gain)
    half_total = TOKEN_TOTAL // TOK_H
    shards = normed.reshape(half_total, TOK_H, D)
    run_ends = jnp.cumsum(class_counts, axis=1)
    starts = run_ends - class_counts
    depth_range = jnp.arange(CAP)
    picked_index = jnp.clip(starts[:, :, None] + depth_range[None, None, :], 0, TOK_H - 1).astype(jnp.int32)
    filled = depth_range[None, None, :] < class_counts[:, :, None]
    blocks = jnp.take_along_axis(shards, picked_index.reshape(half_total, CLASSES * CAP)[:, :, None], axis=1)
    blocks = jnp.where(filled.reshape(half_total, CLASSES * CAP)[:, :, None], blocks, jnp.zeros((), jnp.bfloat16))
    blocks = blocks.reshape(half_total, CLASSES, CAP, D)
    core_hidden = w_gate.shape[2] // N_HEAD

    def per_group(totals, compact_rows):
        gate_weight, up_weight, down_weight, owner_id = compact_rows
        chosen = jnp.take(blocks, owner_id, axis=1).reshape(half_total * CAP, D)
        pair_sum = jnp.zeros((half_total * CAP, D), jnp.float32)
        for core_index in range(N_HEAD):
            lower_edge = core_index * core_hidden
            gate_act = jnp.dot(chosen, gate_weight[:, lower_edge:lower_edge + core_hidden], preferred_element_type=jnp.float32)
            up_act = jnp.dot(chosen, up_weight[:, lower_edge:lower_edge + core_hidden], preferred_element_type=jnp.float32)
            hidden = (jax.nn.silu(gate_act) * up_act).astype(jnp.bfloat16)
            partial_out = jnp.dot(hidden, down_weight[lower_edge:lower_edge + core_hidden, :], preferred_element_type=jnp.float32).astype(jnp.bfloat16)
            pair_sum = pair_sum + partial_out.astype(jnp.float32)
        pair_round = pair_sum.astype(jnp.bfloat16).astype(jnp.float32)
        totals = totals.at[:, owner_id].add(pair_round.reshape(half_total, CAP, D))
        return (totals, None)
    totals = jnp.zeros((half_total, CLASSES, CAP, D), jnp.float32)
    totals, unused_out = lax.scan(per_group, totals, (w_gate, w_up, w_down, owner_class))
    row_range = jnp.arange(TOK_H)
    row_class = lax.optimization_barrier(jnp.sum((row_range[None, :, None] >= run_ends[:, None, :]).astype(jnp.int32), axis=2)).astype(jnp.int32)
    row_start = jnp.take_along_axis(starts, row_class, axis=1)
    gather_index = (row_class * CAP + row_range[None, :] - row_start).astype(jnp.int32)
    ffn_rows = jnp.take_along_axis(totals.reshape(half_total, CLASSES * CAP, D), gather_index[:, :, None], axis=1)
    return (mixed_values + ffn_rows.reshape(TOKEN_TOTAL, D)).astype(jnp.bfloat16)
```

```python
import math

import jax
import jax.numpy as jnp
from jax import lax
from jax.sharding import PartitionSpec as P

HEAD_SIZE = 128


def attend(queries, key_matrix, value_matrix, episode_index):
    length = queries.shape[0]
    kv_count = key_matrix.shape[1] // HEAD_SIZE
    head_repeats = queries.shape[1] // key_matrix.shape[1]
    query_tiles = queries.reshape(length, kv_count, head_repeats, HEAD_SIZE)
    key_tiles = key_matrix.reshape(length, kv_count, HEAD_SIZE)
    value_tiles = value_matrix.reshape(length, kv_count, HEAD_SIZE)
    logit_table = jnp.einsum(
        "envh,ynh->nvey", query_tiles, key_tiles, preferred_element_type=jnp.float32
    )
    logit_table = logit_table * (1.0 / math.sqrt(HEAD_SIZE))
    places = jnp.arange(length)
    allowed = (episode_index[:, None] == episode_index[None, :]) & (
        places[None, :] <= places[:, None]
    )
    logit_table = jnp.where(allowed, logit_table, -jnp.inf)
    softmax_probs = jax.nn.softmax(logit_table, axis=-1).astype(jnp.bfloat16)
    mixed_values = jnp.einsum(
        "alwn,nam->walm", softmax_probs, value_tiles, preferred_element_type=jnp.float32
    )
    return mixed_values.reshape(length, kv_count * head_repeats * HEAD_SIZE).astype(jnp.bfloat16)


def normalize(mixed_values, norm_gain):
    square = jnp.mean(mixed_values * mixed_values, axis=-1, keepdims=True)
    return (mixed_values * lax.rsqrt(square + 1e-06) * norm_gain.astype(jnp.float32)).astype(
        jnp.bfloat16
    )


def class_network(token_block, w_gate, w_up, w_down):
    sources, depth_rows, model_width = token_block.shape
    flattened = token_block.reshape(sources * depth_rows, model_width)
    gate_act = jnp.dot(flattened, w_gate[0], preferred_element_type=jnp.float32)
    up_act = jnp.dot(flattened, w_up[0], preferred_element_type=jnp.float32)
    hidden = (jax.nn.silu(gate_act) * up_act).astype(jnp.bfloat16)
    partial_out = jnp.dot(hidden, w_down[0], preferred_element_type=jnp.float32).astype(
        jnp.bfloat16
    )
    return partial_out.reshape(sources, depth_rows, model_width)


def on_device(
    queries,
    key_matrix,
    value_matrix,
    residual,
    norm_gain,
    w_gate,
    w_up,
    w_down,
    owner_class,
    class_counts,
    episode_index,
):
    local_heads = attend(queries, key_matrix, value_matrix, episode_index)
    attention_output = lax.all_to_all(local_heads, "head", split_axis=0, concat_axis=1, tiled=True)
    mixed_values = residual.astype(jnp.float32) + attention_output.astype(jnp.float32)
    normed = normalize(mixed_values, norm_gain)
    shard_rows = residual.shape[0]
    model_width = residual.shape[1]
    capacity = 3 * shard_rows // 8
    class_total = class_counts.shape[1]
    group_count = owner_class.shape[0]
    core_total = lax.axis_size("head")
    counts = class_counts[0]
    class_range = jnp.arange(class_total)
    run_ends = jnp.sum(
        jnp.where(class_range[None, :] <= class_range[:, None], counts[None, :], 0), axis=1
    )
    starts = run_ends - counts
    owner_table = (owner_class[:, None] == class_range[None, :]).astype(jnp.int32)
    dest_start = jnp.sum(owner_table * starts[None, :], axis=1)
    dest_count = jnp.sum(owner_table * counts[None, :], axis=1)
    depth_range = jnp.arange(capacity)
    picked_index = jnp.clip(dest_start[:, None] + depth_range[None, :], 0, shard_rows - 1)
    filled = depth_range[None, :] < dest_count[:, None]
    outgoing = jnp.take(normed, picked_index.reshape(-1), axis=0).reshape(
        group_count, capacity, model_width
    )
    outgoing = jnp.where(filled[:, :, None], outgoing, jnp.zeros((), jnp.bfloat16))
    arrived = lax.all_to_all(outgoing, "grp", split_axis=0, concat_axis=0, tiled=True)
    token_block = lax.all_gather(arrived, "head", axis=0, tiled=True)
    partial_out = class_network(token_block, w_gate, w_up, w_down)
    halves = lax.all_to_all(partial_out, "head", split_axis=0, concat_axis=0, tiled=True)
    pair_sum = jnp.sum(
        halves.reshape(core_total, group_count, capacity, model_width).astype(jnp.float32), axis=0
    ).astype(jnp.bfloat16)
    returned = lax.all_to_all(pair_sum, "grp", split_axis=0, concat_axis=0, tiled=True)
    owner_weights = owner_table.astype(jnp.bfloat16)
    class_sums = jnp.einsum(
        "sc,sid->cid", owner_weights, returned, preferred_element_type=jnp.float32
    )
    row_range = jnp.arange(shard_rows)
    row_class = jnp.sum((row_range[:, None] >= run_ends[None, :]).astype(jnp.int32), axis=1)
    row_table = (row_class[:, None] == class_range[None, :]).astype(jnp.int32)
    within = row_range - jnp.sum(row_table * starts[None, :], axis=1)
    ffn_rows = jnp.take(
        class_sums.reshape(class_total * capacity, model_width),
        row_class * capacity + within,
        axis=0,
    )
    return (mixed_values + ffn_rows).astype(jnp.bfloat16)


def solution(mesh):
    return jax.shard_map(
        on_device,
        mesh=mesh,
        in_specs=(
            P(("rep", "grp"), "head"),
            P(("rep", "grp"), "head"),
            P(("rep", "grp"), "head"),
            P(("rep", "grp", "head"), None),
            P(),
            P("grp", None, "head"),
            P("grp", None, "head"),
            P("grp", "head", None),
            P(),
            P(("rep", "grp", "head"), None),
            P(("rep", "grp")),
        ),
        out_specs=P(("rep", "grp", "head"), None),
        check_vma=False,
    )
```

```python
import functools
import math

import jax
import jax.numpy as jnp
from jax import lax
from jax.experimental import pallas as pl
from jax.experimental.pallas import tpu as pltpu
from jax.sharding import PartitionSpec as P

HEAD_SIZE = 128


def attend(queries, key_matrix, value_matrix, episode_index):
    length = queries.shape[0]
    kv_count = key_matrix.shape[1] // HEAD_SIZE
    head_repeats = queries.shape[1] // key_matrix.shape[1]
    query_tiles = queries.reshape(length, kv_count, head_repeats, HEAD_SIZE)
    key_tiles = key_matrix.reshape(length, kv_count, HEAD_SIZE)
    value_tiles = value_matrix.reshape(length, kv_count, HEAD_SIZE)
    logit_table = jnp.einsum(
        "envh,ynh->nvey", query_tiles, key_tiles, preferred_element_type=jnp.float32
    )
    logit_table = logit_table * (1.0 / math.sqrt(HEAD_SIZE))
    places = jnp.arange(length)
    allowed = (episode_index[:, None] == episode_index[None, :]) & (
        places[None, :] <= places[:, None]
    )
    logit_table = jnp.where(allowed, logit_table, -jnp.inf)
    softmax_probs = jax.nn.softmax(logit_table, axis=-1).astype(jnp.bfloat16)
    mixed_values = jnp.einsum(
        "alwn,nam->walm", softmax_probs, value_tiles, preferred_element_type=jnp.float32
    )
    return mixed_values.reshape(length, kv_count * head_repeats * HEAD_SIZE).astype(jnp.bfloat16)


def normalize(mixed_values, norm_gain):
    square = jnp.mean(mixed_values * mixed_values, axis=-1, keepdims=True)
    return (mixed_values * lax.rsqrt(square + 1e-06) * norm_gain.astype(jnp.float32)).astype(
        jnp.bfloat16
    )


def exchange_kernel(
    group_total,
    outgoing,
    gate_hbm,
    up_hbm,
    down_hbm,
    answer,
    tokens,
    rows,
    hidden,
    part,
    got,
    pair,
    back,
    gate,
    up,
    down,
    weight_sem,
    own_sem,
    out_send,
    out_recv,
    near_send,
    near_recv,
    part_send,
    part_recv,
    back_send,
    back_recv,
):
    me = lax.axis_index("grp")
    core = lax.axis_index("head")
    other = 1 - core
    capacity, width = outgoing.shape[1], outgoing.shape[2]
    chunks = 2
    per_chunk = group_total // chunks
    block = 2 * capacity
    columns = 256

    def dispatch(k):
        return pltpu.make_async_remote_copy(
            src_ref=outgoing.at[k],
            dst_ref=tokens.at[k, core],
            send_sem=out_send.at[k],
            recv_sem=out_recv.at[k],
            device_id={"grp": lax.rem(me + k, group_total), "head": core},
            device_id_type=pl.DeviceIdType.MESH,
        )

    def forward(k):
        return pltpu.make_async_remote_copy(
            src_ref=tokens.at[k, core],
            dst_ref=tokens.at[k, core],
            send_sem=near_send.at[k],
            recv_sem=near_recv.at[k],
            device_id={"head": other},
            device_id_type=pl.DeviceIdType.MESH,
        )

    def forwarded(k):
        return pltpu.make_async_remote_copy(
            src_ref=tokens.at[k, other],
            dst_ref=tokens.at[k, other],
            send_sem=near_send.at[k],
            recv_sem=near_recv.at[k],
            device_id={"head": other},
            device_id_type=pl.DeviceIdType.MESH,
        )

    def exchange(k):
        return pltpu.make_async_remote_copy(
            src_ref=part.at[k, other],
            dst_ref=got.at[k],
            send_sem=part_send.at[k],
            recv_sem=part_recv.at[k],
            device_id={"head": other},
            device_id_type=pl.DeviceIdType.MESH,
        )

    def give_back(k):
        return pltpu.make_async_remote_copy(
            src_ref=pair.at[k],
            dst_ref=back.at[k],
            send_sem=back_send.at[k],
            recv_sem=back_recv.at[k],
            device_id={"grp": lax.rem(me - k + group_total, group_total), "head": core},
            device_id_type=pl.DeviceIdType.MESH,
        )

    def each(lower, upper, body):
        def step(k, carry):
            body(k)
            return carry

        lax.fori_loop(lower, upper, step, 0)

    loads = [
        pltpu.make_async_copy(src.at[0], dst, weight_sem.at[i])
        for i, (src, dst) in enumerate(((gate_hbm, gate), (up_hbm, up), (down_hbm, down)))
    ]
    for load in loads:
        load.start()
    own = pltpu.make_async_copy(outgoing.at[0], tokens.at[0, core], own_sem)
    own.start()

    barrier = pltpu.get_barrier_semaphore()

    def greet(k):
        pl.semaphore_signal(
            barrier,
            inc=1,
            device_id={"grp": lax.rem(me + k, group_total), "head": core},
            device_id_type=pl.DeviceIdType.MESH,
        )

    each(1, group_total, greet)
    pl.semaphore_signal(
        barrier, inc=1, device_id={"head": other}, device_id_type=pl.DeviceIdType.MESH
    )
    pl.semaphore_wait(barrier, group_total)

    each(1, group_total, lambda k: dispatch(k).start())
    own.wait()
    forward(0).start()

    def relay(k):
        dispatch(k).wait_recv()
        forward(k).start()

    def network(chunk):
        first = chunk * per_chunk

        def gather(i):
            k = first + i
            forwarded(k).wait_recv()
            rows[pl.ds(pl.multiple_of(i * block, block), block), :] = (
                tokens[k].astype(jnp.float32).reshape(block, width).astype(jnp.bfloat16)
            )

        each(0, per_chunk, gather)
        if chunk == 0:
            loads[0].wait()
            loads[1].wait()

        def widen(j):
            span = pl.ds(pl.multiple_of(j * columns, columns), columns)
            gate_act = jnp.dot(rows[...], gate[:, span], preferred_element_type=jnp.float32)
            up_act = jnp.dot(rows[...], up[:, span], preferred_element_type=jnp.float32)
            hidden[:, span] = (gate_act / (1.0 + jnp.exp(-gate_act)) * up_act).astype(jnp.bfloat16)

        each(0, hidden.shape[1] // columns, widen)
        if chunk == 0:
            loads[2].wait()

        def narrow(j):
            span = pl.ds(pl.multiple_of(j * columns, columns), columns)
            total = jnp.dot(hidden[...], down[:, span], preferred_element_type=jnp.float32)
            part[first : first + per_chunk, :, :, span] = total.reshape(
                per_chunk, 2, capacity, columns
            ).astype(jnp.bfloat16)

        each(0, width // columns, narrow)
        each(first, first + per_chunk, lambda k: exchange(k).start())

    def add_pair(k):
        exchange(k).wait_recv()
        pair[k] = (part[k, core].astype(jnp.float32) + got[k].astype(jnp.float32)).astype(
            jnp.bfloat16
        )

    def reply(k):
        add_pair(k)
        give_back(k).start()

    each(1, per_chunk, relay)
    network(0)
    each(per_chunk, group_total, relay)
    add_pair(0)
    each(1, per_chunk, reply)
    network(1)
    each(per_chunk, group_total, reply)

    answer[0] = pair[0]

    def finish(k):
        give_back(k).wait_recv()
        answer[k] = back[k]
        dispatch(k).wait_send()
        give_back(k).wait_send()

    each(1, group_total, finish)

    def drain(k):
        forward(k).wait_send()
        exchange(k).wait_send()

    each(0, group_total, drain)


def exchange_network(outgoing, w_gate, w_up, w_down):
    group_total, capacity, width = outgoing.shape
    units = w_gate.shape[2]
    chunk_rows = group_total * capacity
    anywhere = pl.BlockSpec(memory_space=pl.ANY)
    near = pl.BlockSpec(memory_space=pltpu.VMEM)
    many = pltpu.SemaphoreType.DMA((group_total,))
    return pl.pallas_call(
        functools.partial(exchange_kernel, group_total),
        out_shape=jax.ShapeDtypeStruct(outgoing.shape, jnp.bfloat16),
        in_specs=[near, anywhere, anywhere, anywhere],
        out_specs=near,
        scratch_shapes=[
            pltpu.VMEM((group_total, 2, capacity, width), jnp.bfloat16),
            pltpu.VMEM((chunk_rows, width), jnp.bfloat16),
            pltpu.VMEM((chunk_rows, units), jnp.bfloat16),
            pltpu.VMEM((group_total, 2, capacity, width), jnp.bfloat16),
            pltpu.VMEM((group_total, capacity, width), jnp.bfloat16),
            pltpu.VMEM((group_total, capacity, width), jnp.bfloat16),
            pltpu.VMEM((group_total, capacity, width), jnp.bfloat16),
            pltpu.VMEM(w_gate.shape[1:], jnp.bfloat16),
            pltpu.VMEM(w_up.shape[1:], jnp.bfloat16),
            pltpu.VMEM(w_down.shape[1:], jnp.bfloat16),
            pltpu.SemaphoreType.DMA((3,)),
            pltpu.SemaphoreType.DMA,
            many,
            many,
            many,
            many,
            many,
            many,
            many,
            many,
        ],
        compiler_params=pltpu.CompilerParams(
            collective_id=0, has_side_effects=True, vmem_limit_bytes=60 * 1024 * 1024
        ),
        cost_estimate=pl.CostEstimate(
            flops=12 * chunk_rows * width * units,
            bytes_accessed=6 * width * units,
            transcendentals=2 * chunk_rows * units,
        ),
    )(outgoing, w_gate, w_up, w_down)


def on_device(
    queries,
    key_matrix,
    value_matrix,
    residual,
    norm_gain,
    w_gate,
    w_up,
    w_down,
    owner_class,
    class_counts,
    episode_index,
):
    local_heads = attend(queries, key_matrix, value_matrix, episode_index)
    attention_output = lax.all_to_all(local_heads, "head", split_axis=0, concat_axis=1, tiled=True)
    mixed_values = residual.astype(jnp.float32) + attention_output.astype(jnp.float32)
    normed = normalize(mixed_values, norm_gain)
    shard_rows = residual.shape[0]
    model_width = residual.shape[1]
    capacity = 3 * shard_rows // 8
    class_total = class_counts.shape[1]
    group_count = owner_class.shape[0]
    counts = class_counts[0]
    class_range = jnp.arange(class_total)
    run_ends = jnp.sum(
        jnp.where(class_range[None, :] <= class_range[:, None], counts[None, :], 0), axis=1
    )
    starts = run_ends - counts
    owner_class = jnp.roll(owner_class, -lax.axis_index("grp"))
    owner_table = (owner_class[:, None] == class_range[None, :]).astype(jnp.int32)
    dest_start = jnp.sum(owner_table * starts[None, :], axis=1)
    dest_count = jnp.sum(owner_table * counts[None, :], axis=1)
    depth_range = jnp.arange(capacity)
    picked_index = jnp.clip(dest_start[:, None] + depth_range[None, :], 0, shard_rows - 1)
    filled = depth_range[None, :] < dest_count[:, None]
    outgoing = jnp.take(normed, picked_index.reshape(-1), axis=0).reshape(
        group_count, capacity, model_width
    )
    outgoing = jnp.where(filled[:, :, None], outgoing, jnp.zeros((), jnp.bfloat16))
    returned = exchange_network(outgoing, w_gate, w_up, w_down)
    owner_weights = owner_table.astype(jnp.bfloat16)
    class_sums = jnp.einsum(
        "sc,sid->cid", owner_weights, returned, preferred_element_type=jnp.float32
    )
    row_range = jnp.arange(shard_rows)
    row_class = jnp.sum((row_range[:, None] >= run_ends[None, :]).astype(jnp.int32), axis=1)
    row_table = (row_class[:, None] == class_range[None, :]).astype(jnp.int32)
    within = row_range - jnp.sum(row_table * starts[None, :], axis=1)
    ffn_rows = jnp.take(
        class_sums.reshape(class_total * capacity, model_width),
        row_class * capacity + within,
        axis=0,
    )
    return (mixed_values + ffn_rows).astype(jnp.bfloat16)


def solution(mesh):
    return jax.shard_map(
        on_device,
        mesh=mesh,
        in_specs=(
            P(("rep", "grp"), "head"),
            P(("rep", "grp"), "head"),
            P(("rep", "grp"), "head"),
            P(("rep", "grp", "head"), None),
            P(),
            P("grp", None, "head"),
            P("grp", None, "head"),
            P("grp", "head", None),
            P(),
            P(("rep", "grp", "head"), None),
            P(("rep", "grp")),
        ),
        out_specs=P(("rep", "grp", "head"), None),
        check_vma=False,
    )
```

```python
import functools
import math

import jax
import jax.numpy as jnp
from jax import lax
from jax.experimental import pallas as pl
from jax.experimental.pallas import tpu as pltpu
from jax.sharding import PartitionSpec as P

HEAD_SIZE = 128


def attend(queries, keys, values, episode_column, episode_row, local_heads):
    length = queries.shape[0]
    repeats = queries.shape[1] // keys.shape[1]
    places = lax.broadcasted_iota(jnp.int32, (length, length), 0)
    sources = lax.broadcasted_iota(jnp.int32, (length, length), 1)
    allowed = (episode_column[...] == episode_row[...]) & (sources <= places)
    for j in range(queries.shape[1] // HEAD_SIZE):
        span = slice(j * HEAD_SIZE, (j + 1) * HEAD_SIZE)
        shared = slice(j // repeats * HEAD_SIZE, (j // repeats + 1) * HEAD_SIZE)
        logits = lax.dot_general(
            queries[:, span],
            keys[:, shared],
            (((1,), (1,)), ((), ())),
            preferred_element_type=jnp.float32,
        )
        logits = jnp.where(allowed, logits * (1.0 / math.sqrt(HEAD_SIZE)), -jnp.inf)
        powers = jnp.exp(logits - jnp.max(logits, axis=1, keepdims=True))
        probs = (powers / jnp.sum(powers, axis=1, keepdims=True)).astype(jnp.bfloat16)
        attended = jnp.dot(probs, values[:, shared], preferred_element_type=jnp.float32)
        local_heads[:, :, span] = attended.astype(jnp.bfloat16).reshape(2, length // 2, HEAD_SIZE)


def normalize(residual, mixed, gain, blended, normed):
    half = mixed.shape[2]
    width = 2 * half
    square = 0.0
    for part in range(2):
        span = slice(part * half, (part + 1) * half)
        total = residual[:, span].astype(jnp.float32) + mixed[part].astype(jnp.float32)
        blended[:, span] = total
        square += jnp.sum(total * total, axis=1, keepdims=True)
    scale = lax.rsqrt(square * (1.0 / width) + 1e-06)
    for part in range(2):
        span = slice(part * half, (part + 1) * half)
        normed[:, span] = (
            blended[:, span] * scale * gain[:, span].astype(jnp.float32)
        ).astype(jnp.bfloat16)


def exchange_kernel(
    group_total,
    queries,
    keys,
    values,
    residual,
    gain,
    episode_column,
    episode_row,
    pick,
    merge,
    gate_hbm,
    up_hbm,
    down_hbm,
    result,
    local_heads,
    mixed,
    blended,
    normed,
    outgoing,
    tokens,
    rows,
    hidden,
    part,
    got,
    pair,
    back,
    gate,
    up,
    down,
    weight_sem,
    own_sem,
    out_send,
    out_recv,
    near_send,
    near_recv,
    part_send,
    part_recv,
    back_send,
    back_recv,
    head_send,
    head_recv,
):
    me = lax.axis_index("grp")
    core = lax.axis_index("head")
    other = 1 - core
    capacity, width = outgoing.shape[1], outgoing.shape[2]
    chunks = 2
    per_chunk = group_total // chunks
    block = 2 * capacity
    columns = 256

    def dispatch(k):
        return pltpu.make_async_remote_copy(
            src_ref=outgoing.at[k],
            dst_ref=tokens.at[k, core],
            send_sem=out_send.at[k],
            recv_sem=out_recv.at[k],
            device_id={"grp": lax.rem(me + k, group_total), "head": core},
            device_id_type=pl.DeviceIdType.MESH,
        )

    def forward(k):
        return pltpu.make_async_remote_copy(
            src_ref=tokens.at[k, core],
            dst_ref=tokens.at[k, core],
            send_sem=near_send.at[k],
            recv_sem=near_recv.at[k],
            device_id={"head": other},
            device_id_type=pl.DeviceIdType.MESH,
        )

    def forwarded(k):
        return pltpu.make_async_remote_copy(
            src_ref=tokens.at[k, other],
            dst_ref=tokens.at[k, other],
            send_sem=near_send.at[k],
            recv_sem=near_recv.at[k],
            device_id={"head": other},
            device_id_type=pl.DeviceIdType.MESH,
        )

    def exchange(k):
        return pltpu.make_async_remote_copy(
            src_ref=part.at[k, other],
            dst_ref=got.at[k],
            send_sem=part_send.at[k],
            recv_sem=part_recv.at[k],
            device_id={"head": other},
            device_id_type=pl.DeviceIdType.MESH,
        )

    def give_back(k):
        return pltpu.make_async_remote_copy(
            src_ref=pair.at[k],
            dst_ref=back.at[k],
            send_sem=back_send.at[k],
            recv_sem=back_recv.at[k],
            device_id={"grp": lax.rem(me - k + group_total, group_total), "head": core},
            device_id_type=pl.DeviceIdType.MESH,
        )

    def each(lower, upper, body):
        def step(k, carry):
            body(k)
            return carry

        lax.fori_loop(lower, upper, step, 0)

    loads = [
        pltpu.make_async_copy(src.at[0], dst, weight_sem.at[i])
        for i, (src, dst) in enumerate(((gate_hbm, gate), (up_hbm, up), (down_hbm, down)))
    ]
    for load in loads:
        load.start()

    barrier = pltpu.get_barrier_semaphore()

    def greet(k):
        pl.semaphore_signal(
            barrier,
            inc=1,
            device_id={"grp": lax.rem(me + k, group_total), "head": core},
            device_id_type=pl.DeviceIdType.MESH,
        )

    each(1, group_total, greet)
    pl.semaphore_signal(
        barrier, inc=1, device_id={"head": other}, device_id_type=pl.DeviceIdType.MESH
    )

    attend(queries, keys, values, episode_column, episode_row, local_heads)
    mixed[core] = local_heads[core]
    pl.semaphore_wait(barrier, group_total)
    heads = pltpu.make_async_remote_copy(
        src_ref=local_heads.at[other],
        dst_ref=mixed.at[core],
        send_sem=head_send,
        recv_sem=head_recv,
        device_id={"head": other},
        device_id_type=pl.DeviceIdType.MESH,
    )
    heads.start()
    heads.wait()
    normalize(residual, mixed, gain, blended, normed)

    def choose(j):
        span = pl.ds(pl.multiple_of(j * columns, columns), columns)
        chosen = jnp.dot(pick[...], normed[:, span], preferred_element_type=jnp.float32)
        outgoing[:, :, span] = chosen.reshape(group_total, capacity, columns).astype(jnp.bfloat16)

    each(0, width // columns, choose)
    each(1, group_total, lambda k: dispatch(k).start())
    own = pltpu.make_async_copy(outgoing.at[0], tokens.at[0, core], own_sem)
    own.start()
    own.wait()
    forward(0).start()

    def relay(k):
        dispatch(k).wait_recv()
        forward(k).start()

    def network(chunk):
        first = chunk * per_chunk

        def gather(i):
            k = first + i
            forwarded(k).wait_recv()
            rows[pl.ds(pl.multiple_of(i * block, block), block), :] = (
                tokens[k].astype(jnp.float32).reshape(block, width).astype(jnp.bfloat16)
            )

        each(0, per_chunk, gather)
        if chunk == 0:
            loads[0].wait()
            loads[1].wait()

        def widen(j):
            span = pl.ds(pl.multiple_of(j * columns, columns), columns)
            gate_act = jnp.dot(rows[...], gate[:, span], preferred_element_type=jnp.float32)
            up_act = jnp.dot(rows[...], up[:, span], preferred_element_type=jnp.float32)
            hidden[:, span] = (gate_act / (1.0 + jnp.exp(-gate_act)) * up_act).astype(jnp.bfloat16)

        each(0, hidden.shape[1] // columns, widen)
        if chunk == 0:
            loads[2].wait()

        def narrow(j):
            span = pl.ds(pl.multiple_of(j * columns, columns), columns)
            total = jnp.dot(hidden[...], down[:, span], preferred_element_type=jnp.float32)
            part[first : first + per_chunk, :, :, span] = total.reshape(
                per_chunk, 2, capacity, columns
            ).astype(jnp.bfloat16)

        each(0, width // columns, narrow)
        each(first, first + per_chunk, lambda k: exchange(k).start())

    def add_pair(k):
        exchange(k).wait_recv()
        pair[k] = (part[k, core].astype(jnp.float32) + got[k].astype(jnp.float32)).astype(
            jnp.bfloat16
        )

    def reply(k):
        add_pair(k)
        give_back(k).start()

    each(1, per_chunk, relay)
    network(0)
    each(per_chunk, group_total, relay)
    add_pair(0)
    each(1, per_chunk, reply)
    network(1)
    each(per_chunk, group_total, reply)

    back[0] = pair[0]

    def finish(k):
        give_back(k).wait_recv()
        dispatch(k).wait_send()
        give_back(k).wait_send()

    each(1, group_total, finish)

    def combine(j):
        span = pl.ds(pl.multiple_of(j * columns, columns), columns)
        replies = back[:, :, span].astype(jnp.float32).reshape(group_total * capacity, columns)
        sums = jnp.dot(
            merge[...], replies.astype(jnp.bfloat16), preferred_element_type=jnp.float32
        )
        result[:, span] = (blended[:, span] + sums).astype(jnp.bfloat16)

    each(0, width // columns, combine)

    def drain(k):
        forward(k).wait_send()
        exchange(k).wait_send()

    each(0, group_total, drain)


def layer(arrays, weights, group_total, capacity):
    queries, residual = arrays[0], arrays[3]
    shard_rows, width = residual.shape
    length, half = queries.shape
    units = weights[0].shape[2]
    chunk_rows = group_total * capacity
    near = pl.BlockSpec(memory_space=pltpu.VMEM)
    blocks = pltpu.VMEM((group_total, capacity, width), jnp.bfloat16)
    core_blocks = pltpu.VMEM((group_total, 2, capacity, width), jnp.bfloat16)
    many = pltpu.SemaphoreType.DMA((group_total,))
    return pl.pallas_call(
        functools.partial(exchange_kernel, group_total),
        out_shape=jax.ShapeDtypeStruct(residual.shape, jnp.bfloat16),
        in_specs=[near] * len(arrays) + [pl.BlockSpec(memory_space=pl.ANY)] * 3,
        out_specs=near,
        scratch_shapes=[
            pltpu.VMEM((2, length // 2, half), jnp.bfloat16),
            pltpu.VMEM((2, length // 2, half), jnp.bfloat16),
            pltpu.VMEM((shard_rows, width), jnp.float32),
            pltpu.VMEM((shard_rows, width), jnp.bfloat16),
            blocks,
            core_blocks,
            pltpu.VMEM((chunk_rows, width), jnp.bfloat16),
            pltpu.VMEM((chunk_rows, units), jnp.bfloat16),
            core_blocks,
            blocks,
            blocks,
            blocks,
        ]
        + [pltpu.VMEM(w.shape[1:], jnp.bfloat16) for w in weights]
        + [pltpu.SemaphoreType.DMA((3,)), pltpu.SemaphoreType.DMA]
        + [many] * 8
        + [pltpu.SemaphoreType.DMA] * 2,
        compiler_params=pltpu.CompilerParams(
            collective_id=0, has_side_effects=True, vmem_limit_bytes=60 * 1024 * 1024
        ),
        cost_estimate=pl.CostEstimate(
            flops=12 * chunk_rows * width * units,
            bytes_accessed=6 * width * units,
            transcendentals=2 * chunk_rows * units,
        ),
    )(*arrays, *weights)


def on_device(
    queries,
    key_matrix,
    value_matrix,
    residual,
    norm_gain,
    w_gate,
    w_up,
    w_down,
    owner_class,
    class_counts,
    episode_index,
):
    shard_rows = residual.shape[0]
    capacity = 3 * shard_rows // 8
    class_total = class_counts.shape[1]
    group_count = owner_class.shape[0]
    counts = class_counts[0]
    class_range = jnp.arange(class_total)
    starts = jnp.sum(
        jnp.where(class_range[None, :] < class_range[:, None], counts[None, :], 0), axis=1
    )
    group_range = jnp.arange(group_count)
    dest = (lax.axis_index("grp") + group_range) % group_count
    owner_table = (owner_class[:, None] == class_range[None, :])[None]
    owner_table = owner_table & (dest[:, None] == group_range[None, :])[:, :, None]
    dest_start = jnp.sum(jnp.where(owner_table, starts, 0), axis=(1, 2))
    dest_count = jnp.sum(jnp.where(owner_table, counts, 0), axis=(1, 2))
    depth_range = jnp.arange(capacity)
    row_range = jnp.arange(shard_rows)
    place = jnp.where(
        depth_range[None, :] < dest_count[:, None], dest_start[:, None] + depth_range[None, :], -1
    ).reshape(-1)
    pick = (place[:, None] == row_range[None, :]).astype(jnp.bfloat16)
    merge = (row_range[:, None] == place[None, :]).astype(jnp.bfloat16)
    return layer(
        (
            queries,
            key_matrix,
            value_matrix,
            residual,
            norm_gain[None, :],
            episode_index[:, None],
            episode_index[None, :],
            pick,
            merge,
        ),
        (w_gate, w_up, w_down),
        group_count,
        capacity,
    )


def solution(mesh):
    return jax.shard_map(
        on_device,
        mesh=mesh,
        in_specs=(
            P(("rep", "grp"), "head"),
            P(("rep", "grp"), "head"),
            P(("rep", "grp"), "head"),
            P(("rep", "grp", "head"), None),
            P(),
            P("grp", None, "head"),
            P("grp", None, "head"),
            P("grp", "head", None),
            P(),
            P(("rep", "grp", "head"), None),
            P(("rep", "grp")),
        ),
        out_specs=P(("rep", "grp", "head"), None),
        check_vma=False,
    )
```

```python
import functools
import math

import jax
import jax.numpy as jnp
from jax import lax
from jax.experimental import pallas as pl
from jax.experimental.pallas import tpu as pltpu
from jax.sharding import PartitionSpec as P

HEAD_SIZE = 128


def attend(queries, keys, values, episode_row, local_heads):
    length = queries.shape[0]
    repeats = queries.shape[1] // keys.shape[1]
    places = lax.broadcasted_iota(jnp.int32, (length, length), 0)
    sources = lax.broadcasted_iota(jnp.int32, (length, length), 1)
    episodes = jnp.broadcast_to(episode_row[...], (length, length))
    allowed = (episodes.T == episodes) & (sources <= places)
    for j in range(queries.shape[1] // HEAD_SIZE):
        span = slice(j * HEAD_SIZE, (j + 1) * HEAD_SIZE)
        shared = slice(j // repeats * HEAD_SIZE, (j // repeats + 1) * HEAD_SIZE)
        logits = lax.dot_general(
            queries[:, span],
            keys[:, shared],
            (((1,), (1,)), ((), ())),
            preferred_element_type=jnp.float32,
        )
        logits = jnp.where(allowed, logits * (1.0 / math.sqrt(HEAD_SIZE)), -jnp.inf)
        powers = jnp.exp(logits - jnp.max(logits, axis=1, keepdims=True))
        probs = (powers / jnp.sum(powers, axis=1, keepdims=True)).astype(jnp.bfloat16)
        attended = jnp.dot(probs, values[:, shared], preferred_element_type=jnp.float32)
        local_heads[:, :, span] = attended.astype(jnp.bfloat16).reshape(2, length // 2, HEAD_SIZE)


def normalize(residual, mixed, gain, blended, normed):
    half = mixed.shape[2]
    width = 2 * half
    square = 0.0
    for part in range(2):
        span = slice(part * half, (part + 1) * half)
        total = residual[:, span].astype(jnp.float32) + mixed[part].astype(jnp.float32)
        blended[:, span] = total
        square += jnp.sum(total * total, axis=1, keepdims=True)
    gains = gain[...].astype(jnp.float32)[None, :]
    scale = lax.rsqrt(square * (1.0 / width) + 1e-06)
    for part in range(2):
        span = slice(part * half, (part + 1) * half)
        normed[:, span] = (
            blended[:, span] * scale * gains[:, span]
        ).astype(jnp.bfloat16)


def exchange_kernel(
    group_total,
    queries,
    keys,
    values,
    residual,
    gain,
    episode_row,
    owner_class,
    class_counts,
    gate_hbm,
    up_hbm,
    down_hbm,
    result,
    local_heads,
    mixed,
    blended,
    normed,
    pick,
    merge,
    outgoing,
    tokens,
    rows,
    hidden,
    part,
    got,
    pair,
    back,
    gate,
    up,
    down,
    weight_sem,
    own_sem,
    out_send,
    out_recv,
    near_send,
    near_recv,
    part_send,
    part_recv,
    back_send,
    back_recv,
    head_send,
    head_recv,
):
    me = lax.axis_index("grp")
    core = lax.axis_index("head")
    other = 1 - core
    capacity, width = outgoing.shape[1], outgoing.shape[2]
    half = group_total // 2
    chunks = ((half, half + half // 2), (half + half // 2, group_total), (0, half))
    block = 2 * capacity
    columns = 256

    def partner(k, sign):
        side = lax.rem(me // half + k // half, 2)
        return side * half + lax.rem(lax.rem(me, half) + sign * lax.rem(k, half) + half, half)

    def dispatch(k):
        return pltpu.make_async_remote_copy(
            src_ref=outgoing.at[k],
            dst_ref=tokens.at[k, core],
            send_sem=out_send.at[k],
            recv_sem=out_recv.at[k],
            device_id={"grp": partner(k, 1), "head": core},
            device_id_type=pl.DeviceIdType.MESH,
        )

    def forward(k):
        return pltpu.make_async_remote_copy(
            src_ref=tokens.at[k, core],
            dst_ref=tokens.at[k, core],
            send_sem=near_send.at[k],
            recv_sem=near_recv.at[k],
            device_id={"head": other},
            device_id_type=pl.DeviceIdType.MESH,
        )

    def forwarded(k):
        return pltpu.make_async_remote_copy(
            src_ref=tokens.at[k, other],
            dst_ref=tokens.at[k, other],
            send_sem=near_send.at[k],
            recv_sem=near_recv.at[k],
            device_id={"head": other},
            device_id_type=pl.DeviceIdType.MESH,
        )

    def exchange(k):
        return pltpu.make_async_remote_copy(
            src_ref=part.at[k, other],
            dst_ref=got.at[k],
            send_sem=part_send.at[k],
            recv_sem=part_recv.at[k],
            device_id={"head": other},
            device_id_type=pl.DeviceIdType.MESH,
        )

    def give_back(k):
        return pltpu.make_async_remote_copy(
            src_ref=pair.at[k],
            dst_ref=back.at[k],
            send_sem=back_send.at[k],
            recv_sem=back_recv.at[k],
            device_id={"grp": partner(k, -1), "head": core},
            device_id_type=pl.DeviceIdType.MESH,
        )

    def each(lower, upper, body):
        def step(k, carry):
            body(k)
            return carry

        lax.fori_loop(lower, upper, step, 0)

    loads = [
        pltpu.make_async_copy(src.at[0], dst, weight_sem.at[i])
        for i, (src, dst) in enumerate(((gate_hbm, gate), (up_hbm, up), (down_hbm, down)))
    ]
    for load in loads:
        load.start()

    barrier = pltpu.get_barrier_semaphore()

    def greet(k):
        pl.semaphore_signal(
            barrier,
            inc=1,
            device_id={"grp": partner(k, 1), "head": core},
            device_id_type=pl.DeviceIdType.MESH,
        )

    each(1, group_total, greet)
    pl.semaphore_signal(
        barrier, inc=1, device_id={"head": other}, device_id_type=pl.DeviceIdType.MESH
    )

    depth = lax.broadcasted_iota(jnp.int32, (capacity, residual.shape[0]), 0)
    place = lax.broadcasted_iota(jnp.int32, (capacity, residual.shape[0]), 1)

    def locate(k):
        wanted = owner_class[partner(k, 1)]
        start, count = 0, 0
        for c in range(class_counts.shape[1]):
            start += jnp.where(c < wanted, class_counts[0, c], 0)
            count += jnp.where(c == wanted, class_counts[0, c], 0)
        hot = (place - start == depth) & (depth < count)
        pick[pl.ds(pl.multiple_of(k * capacity, 8), capacity), :] = jnp.where(hot, 1.0, 0.0)

    each(0, group_total, locate)
    merge[...] = pick[...].T.astype(jnp.bfloat16)
    attend(queries, keys, values, episode_row, local_heads)
    mixed[core] = local_heads[core]
    pl.semaphore_wait(barrier, group_total)
    heads = pltpu.make_async_remote_copy(
        src_ref=local_heads.at[other],
        dst_ref=mixed.at[core],
        send_sem=head_send,
        recv_sem=head_recv,
        device_id={"head": other},
        device_id_type=pl.DeviceIdType.MESH,
    )
    heads.start()
    heads.wait()
    normalize(residual, mixed, gain, blended, normed)

    def choose(j):
        span = pl.ds(pl.multiple_of(j * columns, columns), columns)
        chosen = jnp.dot(
            pick[...].astype(jnp.bfloat16), normed[:, span], preferred_element_type=jnp.float32
        )
        outgoing[:, :, span] = chosen.reshape(group_total, capacity, columns).astype(jnp.bfloat16)

    each(0, width // columns, choose)
    each(*chunks[0], lambda k: dispatch(k).start())
    own = pltpu.make_async_copy(outgoing.at[0], tokens.at[0, core], own_sem)
    own.start()
    own.wait()
    forward(0).start()
    each(*chunks[0], lambda k: dispatch(k).wait_send())
    each(*chunks[1], lambda k: dispatch(k).start())
    each(1, half, lambda k: dispatch(k).start())

    def relay(k):
        dispatch(k).wait_recv()
        forward(k).start()

    def network(chunk):
        first, last = chunks[chunk]
        held = (last - first) * block

        def gather(i):
            k = first + i
            forwarded(k).wait_recv()
            rows[pl.ds(pl.multiple_of(i * block, block), block), :] = (
                tokens[k].astype(jnp.float32).reshape(block, width).astype(jnp.bfloat16)
            )

        each(0, last - first, gather)
        if chunk == 0:
            loads[0].wait()
            loads[1].wait()

        def widen(j):
            span = pl.ds(pl.multiple_of(j * columns, columns), columns)
            gate_act = jnp.dot(rows[:held], gate[:, span], preferred_element_type=jnp.float32)
            up_act = jnp.dot(rows[:held], up[:, span], preferred_element_type=jnp.float32)
            hidden[:held, span] = (gate_act / (1.0 + jnp.exp(-gate_act)) * up_act).astype(jnp.bfloat16)

        each(0, hidden.shape[1] // columns, widen)
        if chunk == 0:
            loads[2].wait()

        def narrow(j):
            span = pl.ds(pl.multiple_of(j * columns, columns), columns)
            total = jnp.dot(hidden[:held], down[:, span], preferred_element_type=jnp.float32)
            part[first:last, :, :, span] = total.reshape(
                last - first, 2, capacity, columns
            ).astype(jnp.bfloat16)

        each(0, width // columns, narrow)
        each(first, last, lambda k: exchange(k).start())

    def add_pair(k):
        exchange(k).wait_recv()
        pair[k] = (part[k, core].astype(jnp.float32) + got[k].astype(jnp.float32)).astype(
            jnp.bfloat16
        )

    def reply(k):
        add_pair(k)
        give_back(k).start()

    each(*chunks[0], relay)
    network(0)
    each(*chunks[0], reply)
    each(*chunks[1], relay)
    network(1)
    each(1, half, relay)
    each(*chunks[1], reply)
    network(2)
    each(1, half, reply)
    add_pair(0)

    back[0] = pair[0]

    def finish(k):
        give_back(k).wait_recv()
        give_back(k).wait_send()

    each(1, group_total, finish)
    each(1, half, lambda k: dispatch(k).wait_send())
    each(*chunks[1], lambda k: dispatch(k).wait_send())

    def combine(j):
        span = pl.ds(pl.multiple_of(j * columns, columns), columns)
        replies = back[:, :, span].astype(jnp.float32).reshape(group_total * capacity, columns)
        sums = jnp.dot(
            merge[...], replies.astype(jnp.bfloat16), preferred_element_type=jnp.float32
        )
        result[:, span] = (blended[:, span] + sums).astype(jnp.bfloat16)

    each(0, width // columns, combine)

    def drain(k):
        forward(k).wait_send()
        exchange(k).wait_send()

    each(0, group_total, drain)


def layer(arrays, weights, group_total, capacity):
    queries, residual = arrays[0], arrays[3]
    shard_rows, width = residual.shape
    length, half = queries.shape
    units = weights[0].shape[2]
    chunk_rows = group_total * capacity
    near = pl.BlockSpec(memory_space=pltpu.VMEM)
    blocks = pltpu.VMEM((group_total, capacity, width), jnp.bfloat16)
    core_blocks = pltpu.VMEM((group_total, 2, capacity, width), jnp.bfloat16)
    many = pltpu.SemaphoreType.DMA((group_total,))
    return pl.pallas_call(
        functools.partial(exchange_kernel, group_total),
        out_shape=jax.ShapeDtypeStruct(residual.shape, jnp.bfloat16),
        in_specs=[near] * (len(arrays) - 2)
        + [pl.BlockSpec(memory_space=pltpu.SMEM)] * 2
        + [pl.BlockSpec(memory_space=pl.ANY)] * 3,
        out_specs=near,
        scratch_shapes=[
            pltpu.VMEM((2, length // 2, half), jnp.bfloat16),
            pltpu.VMEM((2, length // 2, half), jnp.bfloat16),
            pltpu.VMEM((shard_rows, width), jnp.float32),
            pltpu.VMEM((shard_rows, width), jnp.bfloat16),
            pltpu.VMEM((chunk_rows, shard_rows), jnp.float32),
            pltpu.VMEM((shard_rows, chunk_rows), jnp.bfloat16),
            blocks,
            core_blocks,
            pltpu.VMEM((chunk_rows, width), jnp.bfloat16),
            pltpu.VMEM((chunk_rows, units), jnp.bfloat16),
            core_blocks,
            blocks,
            blocks,
            blocks,
        ]
        + [pltpu.VMEM(w.shape[1:], jnp.bfloat16) for w in weights]
        + [pltpu.SemaphoreType.DMA((3,)), pltpu.SemaphoreType.DMA]
        + [many] * 8
        + [pltpu.SemaphoreType.DMA] * 2,
        compiler_params=pltpu.CompilerParams(
            collective_id=0, has_side_effects=True, vmem_limit_bytes=60 * 1024 * 1024
        ),
        cost_estimate=pl.CostEstimate(
            flops=12 * chunk_rows * width * units,
            bytes_accessed=6 * width * units,
            transcendentals=2 * chunk_rows * units,
        ),
    )(*arrays, *weights)


def on_device(
    queries,
    key_matrix,
    value_matrix,
    residual,
    norm_gain,
    w_gate,
    w_up,
    w_down,
    owner_class,
    class_counts,
    episode_index,
):
    shard_rows = residual.shape[0]
    capacity = 3 * shard_rows // 8
    group_count = owner_class.shape[0]
    return layer(
        (
            queries,
            key_matrix,
            value_matrix,
            residual,
            norm_gain,
            episode_index[None, :],
            owner_class,
            class_counts,
        ),
        (w_gate, w_up, w_down),
        group_count,
        capacity,
    )


def solution(mesh):
    return jax.shard_map(
        on_device,
        mesh=mesh,
        in_specs=(
            P(("rep", "grp"), "head"),
            P(("rep", "grp"), "head"),
            P(("rep", "grp"), "head"),
            P(("rep", "grp", "head"), None),
            P(),
            P("grp", None, "head"),
            P("grp", None, "head"),
            P("grp", "head", None),
            P(),
            P(("rep", "grp", "head"), None),
            P(("rep", "grp")),
        ),
        out_specs=P(("rep", "grp", "head"), None),
        check_vma=False,
    )
```

```python
import functools
import math

import jax
import jax.numpy as jnp
from jax import lax
from jax.experimental import pallas as pl
from jax.experimental.pallas import tpu as pltpu
from jax.sharding import PartitionSpec as P

HEAD_SIZE = 128


def attend(queries, keys, values, episode_row, local_heads):
    length = queries.shape[0]
    repeats = queries.shape[1] // keys.shape[1]
    places = lax.broadcasted_iota(jnp.int32, (length, length), 0)
    sources = lax.broadcasted_iota(jnp.int32, (length, length), 1)
    episodes = jnp.broadcast_to(episode_row[...], (length, length))
    allowed = (episodes.T == episodes) & (sources <= places)
    for j in range(queries.shape[1] // HEAD_SIZE):
        span = slice(j * HEAD_SIZE, (j + 1) * HEAD_SIZE)
        shared = slice(j // repeats * HEAD_SIZE, (j // repeats + 1) * HEAD_SIZE)
        logits = lax.dot_general(
            queries[:, span],
            keys[:, shared],
            (((1,), (1,)), ((), ())),
            preferred_element_type=jnp.float32,
        )
        logits = jnp.where(allowed, logits * (1.0 / math.sqrt(HEAD_SIZE)), -jnp.inf)
        powers = jnp.exp(logits - jnp.max(logits, axis=1, keepdims=True))
        probs = (powers / jnp.sum(powers, axis=1, keepdims=True)).astype(jnp.bfloat16)
        attended = jnp.dot(probs, values[:, shared], preferred_element_type=jnp.float32)
        local_heads[:, :, span] = attended.astype(jnp.bfloat16).reshape(2, length // 2, HEAD_SIZE)


def normalize(residual, mixed, gain, blended, normed):
    half = mixed.shape[2]
    width = 2 * half
    square = 0.0
    for part in range(2):
        span = slice(part * half, (part + 1) * half)
        total = residual[:, span].astype(jnp.float32) + mixed[part].astype(jnp.float32)
        blended[:, span] = total
        square += jnp.sum(total * total, axis=1, keepdims=True)
    gains = gain[...].astype(jnp.float32)[None, :]
    scale = lax.rsqrt(square * (1.0 / width) + 1e-06)
    for part in range(2):
        span = slice(part * half, (part + 1) * half)
        normed[:, span] = (
            blended[:, span] * scale * gains[:, span]
        ).astype(jnp.bfloat16)


def exchange_kernel(
    group_total,
    queries,
    keys,
    values,
    residual,
    gain,
    episode_row,
    owner_class,
    class_counts,
    gate_hbm,
    up_hbm,
    down_hbm,
    result,
    local_heads,
    mixed,
    blended,
    normed,
    pick,
    merge,
    outgoing,
    tokens,
    rows,
    hidden,
    part,
    got,
    pair,
    back,
    gate,
    up,
    down,
    weight_sem,
    own_sem,
    out_send,
    out_recv,
    near_send,
    near_recv,
    part_send,
    part_recv,
    back_send,
    back_recv,
    head_send,
    head_recv,
):
    me = lax.axis_index("grp")
    core = lax.axis_index("head")
    other = 1 - core
    capacity, width = outgoing.shape[1], outgoing.shape[2]
    half = group_total // 2
    chunks = ((half, half + half // 2), (half + half // 2, group_total), (0, half))
    block = 2 * capacity
    columns = 512
    narrow_columns = width // 2

    def partner(k, sign):
        side = lax.rem(me // half + k // half, 2)
        return side * half + lax.rem(lax.rem(me, half) + sign * lax.rem(k, half) + half, half)

    def dispatch(k):
        return pltpu.make_async_remote_copy(
            src_ref=outgoing.at[k],
            dst_ref=tokens.at[k, core],
            send_sem=out_send.at[k],
            recv_sem=out_recv.at[k],
            device_id={"grp": partner(k, 1), "head": core},
            device_id_type=pl.DeviceIdType.MESH,
        )

    def forward(k):
        return pltpu.make_async_remote_copy(
            src_ref=tokens.at[k, core],
            dst_ref=tokens.at[k, core],
            send_sem=near_send.at[k],
            recv_sem=near_recv.at[k],
            device_id={"head": other},
            device_id_type=pl.DeviceIdType.MESH,
        )

    def forwarded(k):
        return pltpu.make_async_remote_copy(
            src_ref=tokens.at[k, other],
            dst_ref=tokens.at[k, other],
            send_sem=near_send.at[k],
            recv_sem=near_recv.at[k],
            device_id={"head": other},
            device_id_type=pl.DeviceIdType.MESH,
        )

    def exchange(k):
        return pltpu.make_async_remote_copy(
            src_ref=part.at[k, other],
            dst_ref=got.at[k],
            send_sem=part_send.at[k],
            recv_sem=part_recv.at[k],
            device_id={"head": other},
            device_id_type=pl.DeviceIdType.MESH,
        )

    def give_back(k):
        return pltpu.make_async_remote_copy(
            src_ref=pair.at[k],
            dst_ref=back.at[k],
            send_sem=back_send.at[k],
            recv_sem=back_recv.at[k],
            device_id={"grp": partner(k, -1), "head": core},
            device_id_type=pl.DeviceIdType.MESH,
        )

    def each(lower, upper, body):
        def step(k, carry):
            body(k)
            return carry

        lax.fori_loop(lower, upper, step, 0)

    loads = [
        pltpu.make_async_copy(src.at[0], dst, weight_sem.at[i])
        for i, (src, dst) in enumerate(((gate_hbm, gate), (up_hbm, up), (down_hbm, down)))
    ]
    for load in loads:
        load.start()

    barrier = pltpu.get_barrier_semaphore()

    def greet(k):
        pl.semaphore_signal(
            barrier,
            inc=1,
            device_id={"grp": partner(k, 1), "head": core},
            device_id_type=pl.DeviceIdType.MESH,
        )

    each(1, group_total, greet)
    pl.semaphore_signal(
        barrier, inc=1, device_id={"head": other}, device_id_type=pl.DeviceIdType.MESH
    )

    depth = lax.broadcasted_iota(jnp.int32, (capacity, residual.shape[0]), 0)
    place = lax.broadcasted_iota(jnp.int32, (capacity, residual.shape[0]), 1)

    def locate(k):
        wanted = owner_class[partner(k, 1)]
        start, count = 0, 0
        for c in range(class_counts.shape[1]):
            start += jnp.where(c < wanted, class_counts[0, c], 0)
            count += jnp.where(c == wanted, class_counts[0, c], 0)
        hot = (place - start == depth) & (depth < count)
        pick[pl.ds(pl.multiple_of(k * capacity, 8), capacity), :] = jnp.where(hot, 1.0, 0.0)

    each(0, group_total, locate)
    merge[...] = pick[...].T.astype(jnp.bfloat16)
    attend(queries, keys, values, episode_row, local_heads)
    mixed[core] = local_heads[core]
    pl.semaphore_wait(barrier, group_total)
    heads = pltpu.make_async_remote_copy(
        src_ref=local_heads.at[other],
        dst_ref=mixed.at[core],
        send_sem=head_send,
        recv_sem=head_recv,
        device_id={"head": other},
        device_id_type=pl.DeviceIdType.MESH,
    )
    heads.start()
    heads.wait()
    normalize(residual, mixed, gain, blended, normed)

    def choose(j):
        span = pl.ds(pl.multiple_of(j * columns, columns), columns)
        chosen = jnp.dot(
            pick[...].astype(jnp.bfloat16), normed[:, span], preferred_element_type=jnp.float32
        )
        outgoing[:, :, span] = chosen.reshape(group_total, capacity, columns).astype(jnp.bfloat16)

    each(0, width // columns, choose)
    each(*chunks[0], lambda k: dispatch(k).start())
    own = pltpu.make_async_copy(outgoing.at[0], tokens.at[0, core], own_sem)
    own.start()
    own.wait()
    forward(0).start()
    each(*chunks[0], lambda k: dispatch(k).wait_send())
    each(*chunks[1], lambda k: dispatch(k).start())
    each(1, half, lambda k: dispatch(k).start())

    def relay(k):
        dispatch(k).wait_recv()
        forward(k).start()

    def network(chunk):
        first, last = chunks[chunk]
        held = (last - first) * block

        def gather(i):
            k = first + i
            forwarded(k).wait_recv()
            rows[pl.ds(pl.multiple_of(i * block, block), block), :] = (
                tokens[k].astype(jnp.float32).reshape(block, width).astype(jnp.bfloat16)
            )

        each(0, last - first, gather)
        if chunk == 0:
            loads[0].wait()
            loads[1].wait()

        def widen(j):
            span = pl.ds(pl.multiple_of(j * columns, columns), columns)
            gate_act = jnp.dot(rows[:held], gate[:, span], preferred_element_type=jnp.float32)
            up_act = jnp.dot(rows[:held], up[:, span], preferred_element_type=jnp.float32)
            hidden[:held, span] = (gate_act / (1.0 + jnp.exp(-gate_act)) * up_act).astype(jnp.bfloat16)

        each(0, hidden.shape[1] // columns, widen)
        if chunk == 0:
            loads[2].wait()

        def narrow(j):
            span = pl.ds(pl.multiple_of(j * narrow_columns, narrow_columns), narrow_columns)
            total = jnp.dot(hidden[:held], down[:, span], preferred_element_type=jnp.float32)
            part[first:last, :, :, span] = total.reshape(
                last - first, 2, capacity, narrow_columns
            ).astype(jnp.bfloat16)

        each(0, width // narrow_columns, narrow)
        each(first, last, lambda k: exchange(k).start())

    def add_pair(k):
        exchange(k).wait_recv()
        pair[k] = (part[k, core].astype(jnp.float32) + got[k].astype(jnp.float32)).astype(
            jnp.bfloat16
        )

    def reply(k):
        add_pair(k)
        give_back(k).start()

    each(*chunks[0], relay)
    network(0)
    each(*chunks[0], reply)
    each(*chunks[1], relay)
    network(1)
    each(1, half, relay)
    each(*chunks[1], reply)
    network(2)
    each(1, half, reply)
    add_pair(0)

    back[0] = pair[0]

    def finish(k):
        give_back(k).wait_recv()
        give_back(k).wait_send()

    each(1, group_total, finish)
    each(1, half, lambda k: dispatch(k).wait_send())
    each(*chunks[1], lambda k: dispatch(k).wait_send())

    def combine(j):
        span = pl.ds(pl.multiple_of(j * columns, columns), columns)
        replies = back[:, :, span].astype(jnp.float32).reshape(group_total * capacity, columns)
        sums = jnp.dot(
            merge[...], replies.astype(jnp.bfloat16), preferred_element_type=jnp.float32
        )
        result[:, span] = (blended[:, span] + sums).astype(jnp.bfloat16)

    each(0, width // columns, combine)

    def drain(k):
        forward(k).wait_send()
        exchange(k).wait_send()

    each(0, group_total, drain)


def layer(arrays, weights, group_total, capacity):
    queries, residual = arrays[0], arrays[3]
    shard_rows, width = residual.shape
    length, half = queries.shape
    units = weights[0].shape[2]
    chunk_rows = group_total * capacity
    near = pl.BlockSpec(memory_space=pltpu.VMEM)
    blocks = pltpu.VMEM((group_total, capacity, width), jnp.bfloat16)
    core_blocks = pltpu.VMEM((group_total, 2, capacity, width), jnp.bfloat16)
    many = pltpu.SemaphoreType.DMA((group_total,))
    return pl.pallas_call(
        functools.partial(exchange_kernel, group_total),
        out_shape=jax.ShapeDtypeStruct(residual.shape, jnp.bfloat16),
        in_specs=[near] * (len(arrays) - 2)
        + [pl.BlockSpec(memory_space=pltpu.SMEM)] * 2
        + [pl.BlockSpec(memory_space=pl.ANY)] * 3,
        out_specs=near,
        scratch_shapes=[
            pltpu.VMEM((2, length // 2, half), jnp.bfloat16),
            pltpu.VMEM((2, length // 2, half), jnp.bfloat16),
            pltpu.VMEM((shard_rows, width), jnp.float32),
            pltpu.VMEM((shard_rows, width), jnp.bfloat16),
            pltpu.VMEM((chunk_rows, shard_rows), jnp.float32),
            pltpu.VMEM((shard_rows, chunk_rows), jnp.bfloat16),
            blocks,
            core_blocks,
            pltpu.VMEM((chunk_rows, width), jnp.bfloat16),
            pltpu.VMEM((chunk_rows, units), jnp.bfloat16),
            core_blocks,
            blocks,
            blocks,
            blocks,
        ]
        + [pltpu.VMEM(w.shape[1:], jnp.bfloat16) for w in weights]
        + [pltpu.SemaphoreType.DMA((3,)), pltpu.SemaphoreType.DMA]
        + [many] * 8
        + [pltpu.SemaphoreType.DMA] * 2,
        compiler_params=pltpu.CompilerParams(
            collective_id=0, has_side_effects=True, vmem_limit_bytes=60 * 1024 * 1024
        ),
        cost_estimate=pl.CostEstimate(
            flops=12 * chunk_rows * width * units,
            bytes_accessed=6 * width * units,
            transcendentals=2 * chunk_rows * units,
        ),
    )(*arrays, *weights)


def on_device(
    queries,
    key_matrix,
    value_matrix,
    residual,
    norm_gain,
    w_gate,
    w_up,
    w_down,
    owner_class,
    class_counts,
    episode_index,
):
    shard_rows = residual.shape[0]
    capacity = 3 * shard_rows // 8
    group_count = owner_class.shape[0]
    return layer(
        (
            queries,
            key_matrix,
            value_matrix,
            residual,
            norm_gain,
            episode_index[None, :],
            owner_class,
            class_counts,
        ),
        (w_gate, w_up, w_down),
        group_count,
        capacity,
    )


def solution(mesh):
    return jax.shard_map(
        on_device,
        mesh=mesh,
        in_specs=(
            P(("rep", "grp"), "head"),
            P(("rep", "grp"), "head"),
            P(("rep", "grp"), "head"),
            P(("rep", "grp", "head"), None),
            P(),
            P("grp", None, "head"),
            P("grp", None, "head"),
            P("grp", "head", None),
            P(),
            P(("rep", "grp", "head"), None),
            P(("rep", "grp")),
        ),
        out_specs=P(("rep", "grp", "head"), None),
        check_vma=False,
    )
```
